32 devices in a mesh: cuts: 2 (over core), tile: 16 (over z, y, x).
Axes of the slice: x: 2, y: 2, z: 4, core: 2. Of those that a mesh axis runs over, the one named last changes fastest.
Arguments:
- object_slices: float32 [2, 2, 2048, 2048], P('cuts', None, 'tile'), may hold values from -1 to 1, as said below
- probe: float32 [2, 256, 256], replicated, may hold values from -4 to 4
- positions: int32 [32, 2], P('tile'), may hold values from 0 to 1792, as said below
- counts: int32 [16], P('tile'), may hold values from 1 to 2
- intensity: float32 [32, 256, 256], P('tile'), may hold values from 0 to 2
Outputs:
- object_grad: float32 [2, 2, 2048, 2048], P('cuts', None, 'tile')
The draws below stay inside these ranges and needn't reach their ends.
Inputs may be any that keep to these rules, and one draw needn't show every extreme that they name: `positions`: slot s belongs to strip t = s // 2; its row offset lies between max(0, (t - 1) * 128) and min(t * 128, 1792), its column offset between 0 and 1792. `object_slices`: every object cell has a magnitude between 0.7 and 1.0.
All inputs are finite; a program needn't handle non-finite values.
Results may differ from the reference program's by a relative error of at most 0.00015.
Values sent between devices are 32-bit elements; how exact they have to be, the bound alone decides.
A program may use at most 64 MiB of HBM per device.

```python
import math
import jax
import jax.numpy as jnp
from jax import lax

WIN = 256
STRIP = 128
NCOL = 2048
POS_CAP = 2
TILES = 16
SLICES = 2
NROW = 2048
SLOTS = 32


def draw_object_slices(key, part):
    amp_key, phase_key = jax.random.split(jax.random.fold_in(key, 11))
    shape = (SLICES, NROW, NCOL)
    amplitude = jax.random.uniform(amp_key, shape, jnp.float32, 0.75, 1.0)
    phase = jax.random.uniform(phase_key, shape, jnp.float32, -math.pi, math.pi)
    return jnp.stack([amplitude * jnp.cos(phase), amplitude * jnp.sin(phase)], axis=1)


def draw_positions(key, part):
    row_key, col_key, pick_key = jax.random.split(jax.random.fold_in(key, 23), 3)
    owner = jnp.arange(SLOTS, dtype=jnp.int32) // POS_CAP
    lowest = jnp.maximum(0, (owner - 1) * STRIP)
    highest = jnp.minimum(owner * STRIP, NROW - WIN)
    raw_rows = jax.random.randint(row_key, (SLOTS,), 0, STRIP + 1, dtype=jnp.int32)
    row_starts = lowest + raw_rows % (highest - lowest + 1)
    col_starts = jax.random.randint(col_key, (SLOTS,), 0, NCOL - WIN + 1, dtype=jnp.int32)
    chosen = jax.random.permutation(pick_key, SLOTS)
    col_starts = col_starts.at[chosen[0]].set(0).at[chosen[1]].set(NCOL - WIN)
    return jnp.stack([row_starts, col_starts], axis=1)


def draw_counts(key, part):
    base_key, pick_key = jax.random.split(jax.random.fold_in(key, 37))
    drawn = jax.random.randint(base_key, (TILES,), 1, POS_CAP // 2 + 1, dtype=jnp.int32)
    busiest = jax.random.randint(pick_key, (), 0, TILES, dtype=jnp.int32)
    return drawn.at[busiest].set(POS_CAP)


def shard_levels(key, extent, cuts, smallest, top_value):
    gain = 1.0
    for dim, parts in cuts:
        draws = jax.random.uniform(jax.random.fold_in(jax.random.fold_in(key, 6), dim), (parts,), jnp.float32, smallest / len(cuts), top_value / len(cuts))
        gain = gain * jnp.repeat(jnp.exp(draws), extent[dim] // parts).reshape((-1,) + (1,) * (len(extent) - 1 - dim))
    return gain


def scatter_about(own_key, extent, scale, bound, kind=jnp.bfloat16):
    values = scale * jax.random.normal(own_key, extent, jnp.float32)
    return jnp.clip(values, min=-bound, max=bound).astype(kind)


def setup_inputs(seed: int = 0) -> dict:
    streams_of = jax.random.split(jax.random.key(seed), 6)
    object_slices = draw_object_slices(jax.random.fold_in(streams_of[5], 71), 0)
    probe = scatter_about(streams_of[1], (2, WIN, WIN), 0.7, 4.0, jnp.float32)
    positions = draw_positions(jax.random.fold_in(streams_of[5], 71), 0)
    counts = draw_counts(jax.random.fold_in(streams_of[5], 71), 0)
    intensity = jnp.clip(2.0 * jax.random.uniform(streams_of[4], (SLOTS, WIN, WIN), jnp.float32) ** shard_levels(streams_of[4], (SLOTS, WIN, WIN), ((0, 16),), -0.2, 0.2), 0.0, 2.0)
    return dict(object_slices=object_slices, probe=probe, positions=positions, counts=counts, intensity=intensity)


def kernel_phase(window):
    frequency = jnp.arange(window, dtype=jnp.int32)
    centred = (frequency + window // 2) % window - window // 2
    wrapped = (centred * centred) % (4 * window)
    return wrapped.astype(jnp.float32) * (math.pi / (2 * window))


def reference(object_slices, probe, positions, counts, intensity):
    angle = kernel_phase(WIN)
    filter_one = lax.complex(jnp.cos(angle), -jnp.sin(angle))
    filter_two = filter_one[:, None] * filter_one[None, :]
    probe_field = lax.complex(probe[0], probe[1])
    object_field = lax.complex(object_slices[:, 0], object_slices[:, 1])

    def forward_prop(field_in):
        return jnp.fft.ifft2(jnp.fft.fft2(field_in) * filter_two)

    def adjoint_prop(field_in):
        return jnp.fft.ifft2(jnp.fft.fft2(field_in) * jnp.conj(filter_two))

    def one_slot(slot_index, gradient):
        row_start = positions[slot_index, 0].astype(jnp.int32)
        col_start = positions[slot_index, 1].astype(jnp.int32)
        live_weight = (slot_index % POS_CAP < counts[slot_index // POS_CAP]).astype(jnp.float32)
        start = (jnp.int32(0), row_start, col_start)
        patches = lax.dynamic_slice(object_field, start, (SLICES, WIN, WIN))
        wave_now = probe_field
        entering = []
        for layer in range(SLICES):
            entering.append(wave_now)
            wave_now = wave_now * patches[layer]
            if layer + 1 < SLICES:
                wave_now = forward_prop(wave_now)
        far_field = jnp.fft.fft2(wave_now, norm="ortho")
        modelled = jnp.real(far_field) ** 2 + jnp.imag(far_field) ** 2
        residual = (modelled - intensity[slot_index]) * live_weight
        back_wave = jnp.fft.ifft2(far_field * residual, norm="ortho")
        terms = []
        for layer in reversed(range(SLICES)):
            terms.append(jnp.conj(entering[layer]) * back_wave)
            back_wave = jnp.conj(patches[layer]) * back_wave
            if layer > 0:
                back_wave = adjoint_prop(back_wave)
        stacked = jnp.stack(terms[::-1])
        current = lax.dynamic_slice(gradient, start, (SLICES, WIN, WIN))
        return lax.dynamic_update_slice(gradient, current + stacked, start)

    gradient = lax.fori_loop(0, positions.shape[0], one_slot, jnp.zeros_like(object_field))
    return jnp.stack([jnp.real(gradient), jnp.imag(gradient)], axis=1)
```

```python
import functools
import math

import jax
import jax.numpy as jnp
import ml_dtypes
import numpy as np
from jax import lax
from jax.experimental import pallas as pl
from jax.experimental.pallas import tpu as pltpu
from jax.sharding import PartitionSpec as P

MESH = pl.DeviceIdType.MESH
LANES = 128


def split_table(table):
    high = table.astype(ml_dtypes.bfloat16)
    low = (table - high.astype(np.float64)).astype(ml_dtypes.bfloat16)
    return np.stack([high, low])


def build_tables(window):
    counter = np.arange(window)
    turned = (counter[:, None] * counter[None, :] % window) * (2.0 * math.pi / window)
    dft = np.exp(-1j * turned) / math.sqrt(window)
    centred = (counter + window // 2) % window - window // 2
    angle = (centred * centred % (4 * window)) * (math.pi / (2 * window))
    prop = (np.conj(dft) * np.exp(-1j * angle)[None, :]) @ dft

    def right(matrix):
        return np.block([[matrix.real, matrix.imag], [-matrix.imag, matrix.real]])

    return np.stack(
        [split_table(m) for w in (dft, prop) for m in (right(w), right(w).T)]
    )


def halves(value):
    high = value.astype(jnp.bfloat16)
    return high, (value - high.astype(jnp.float32)).astype(jnp.bfloat16)


def dot(left, right):
    return jnp.dot(left, right, preferred_element_type=jnp.float32)


def sandwich(real_in, imag_in, table, right, left):
    window = real_in.shape[0]
    high, low = halves(jnp.concatenate([real_in, imag_in], axis=1))
    middle = dot(high, table[right, 0]) + (dot(low, table[right, 0]) + dot(high, table[right, 1]))
    stacked = jnp.concatenate([middle[:, :window], middle[:, window:]], axis=0)
    high, low = halves(stacked)
    final = dot(table[left, 0], high) + (dot(table[left, 0], low) + dot(table[left, 1], high))
    return final[:window], final[window:]


def roll_kernel(rows, pos, probe, rolled):
    core = lax.axis_index("cuts")
    window = probe.shape[1]
    row = jnp.where(core == 0, pos[0, 0], pos[1, 0]) - (lax.axis_index("tile") - 1) * rows
    row = jnp.clip(row, 0, rows)
    turn = jnp.clip(jnp.where(core == 0, pos[0, 1], pos[1, 1]), 0) % window
    for part in range(2):
        rolled[part] = pltpu.roll(pltpu.roll(probe[part], row, 0), turn, 1)


def cut_kernel(strip, starts, cut):
    blocks = strip.shape[2] // LANES
    lane_row = lax.broadcasted_iota(jnp.int32, (1, LANES), 1)
    for item in range(6):
        start = jnp.full((1, LANES), starts[item], jnp.int32)
        for half in range(2):
            order = list(range(half, blocks, 2))[::-1]
            for part in range(2):
                value = strip[part, :, order[0] * LANES : (order[0] + 1) * LANES]
                for block in order[1:]:
                    value = jnp.where(
                        lane_row + block * LANES >= start,
                        strip[part, :, block * LANES : (block + 1) * LANES],
                        value,
                    )
                cut[item, part, :, half * LANES : (half + 1) * LANES] = value


def wave_kernel(row_ref, live_ref, win, probe, intensity, table, grad):
    rows, window = win.shape[3:]
    row = row_ref[0]
    from_high = lax.broadcasted_iota(jnp.int32, (rows, window), 0) < row

    def object_part(section, part):
        outer = jnp.where(from_high, win[section, 2, part], win[section, 0, part])
        return jnp.concatenate([outer, win[section, 1, part]], axis=0)

    def give_back(section, real_part, imag_part):
        for part, value in ((0, real_part), (1, imag_part)):
            outer = value[:rows]
            grad[section, 0, part] = jnp.where(from_high, 0.0, outer)
            grad[section, 1, part] = value[rows:]
            grad[section, 2, part] = jnp.where(from_high, outer, 0.0)

    probe_re, probe_im = probe[0], probe[1]
    obj_re, obj_im = object_part(0, 0), object_part(0, 1)
    wave_re, wave_im = sandwich(
        probe_re * obj_re - probe_im * obj_im, probe_re * obj_im + probe_im * obj_re, table, 2, 3
    )
    obj_re, obj_im = object_part(1, 0), object_part(1, 1)
    far_re, far_im = sandwich(
        wave_re * obj_re - wave_im * obj_im, wave_re * obj_im + wave_im * obj_re, table, 0, 1
    )
    residual = live_ref[0] * (far_re * far_re + far_im * far_im - intensity[...])
    back_re, back_im = sandwich(residual * far_re, residual * far_im, table, 1, 0)
    give_back(1, wave_re * back_re + wave_im * back_im, wave_re * back_im - wave_im * back_re)
    back_re, back_im = sandwich(
        obj_re * back_re + obj_im * back_im, obj_re * back_im - obj_im * back_re, table, 3, 2
    )
    give_back(0, probe_re * back_re + probe_im * back_im, probe_re * back_im - probe_im * back_re)


def sum_kernel(starts, back, summed):
    rows, window = back.shape[2:]
    blocks = summed.shape[2] // LANES
    lane_row = lax.broadcasted_iota(jnp.int32, (1, LANES), 1)
    for block in range(blocks):
        half = slice((block % 2) * LANES, (block % 2 + 1) * LANES)
        for part in range(2):
            total = jnp.zeros((rows, LANES), jnp.float32)
            for item in range(6):
                offset = lane_row + block * LANES - jnp.full((1, LANES), starts[item], jnp.int32)
                inside = jnp.logical_and(offset >= 0, offset < window)
                total += jnp.where(inside, back[item, part, :, half], 0.0)
            summed[part, :, block * LANES : (block + 1) * LANES] = total


def solution(mesh):
    tiles = mesh.shape["tile"]
    up = [(t, t + 1) for t in range(tiles - 1)]
    down = [(t + 1, t) for t in range(tiles - 1)]
    swap = [(0, 1), (1, 0)]

    def crossed(pairs):
        return [(c * tiles + a, (1 - c) * tiles + b) for c in range(2) for a, b in pairs]

    def call(body, shape, scalars, arrays):
        return pl.pallas_call(
            body,
            out_shape=jax.ShapeDtypeStruct(shape, jnp.float32),
            in_specs=[
                pl.BlockSpec(memory_space=pltpu.SMEM if scalar else pltpu.VMEM)
                for scalar in scalars
            ],
            out_specs=pl.BlockSpec(memory_space=pltpu.VMEM),
            compiler_params=pltpu.CompilerParams(vmem_limit_bytes=40 * 1024 * 1024),
        )(*arrays)

    def exchange(low, own, high):
        core = lax.axis_index("cuts")

        def pick(pieces, same):
            first = (core == 0) == same
            return jnp.where(first, pieces[0], pieces[1])

        both = ("cuts", "tile")
        same = [
            lax.ppermute(pick(high, True), "tile", up),
            pick(own, True),
            lax.ppermute(pick(low, True), "tile", down),
        ]
        other = [
            lax.ppermute(pick(high, False), both, crossed(up)),
            lax.ppermute(pick(own, False), "cuts", swap),
            lax.ppermute(pick(low, False), both, crossed(down)),
        ]
        from_zero = [jnp.where(core == 0, s, o) for s, o in zip(same, other)]
        from_one = [jnp.where(core == 0, o, s) for s, o in zip(same, other)]
        return from_zero, from_one

    def local(object_slices, probe, positions, counts, intensity):
        window = probe.shape[-1]
        rows, ncolumns = object_slices.shape[2:]
        table = jnp.asarray(build_tables(window))
        core = lax.axis_index("cuts")
        below = lax.ppermute(positions, "tile", up)
        above = lax.ppermute(positions, "tile", down)
        starts = jnp.concatenate([below[:, 1], positions[:, 1], above[:, 1]])
        cut = call(
            cut_kernel, (6, 2, rows, window), (False, True), (object_slices[0], starts)
        )
        zero, one = exchange((cut[0], cut[1]), (cut[2], cut[3]), (cut[4], cut[5]))
        win = jnp.stack([jnp.stack(zero), jnp.stack(one)])
        rolled = call(
            functools.partial(roll_kernel, rows), probe.shape, (True, False), (positions, probe)
        )
        row = lax.dynamic_slice(positions[:, 0], (core,), (1,))
        row = row - (lax.axis_index("tile") - 1) * rows
        live = (core < counts).astype(jnp.float32)
        shot = lax.dynamic_index_in_dim(intensity, core, 0, keepdims=False)
        grad = call(
            wave_kernel,
            (2, 3, 2, rows, window),
            (True, True, False, False, False, False),
            (row, live, win, rolled, shot, table),
        )
        zero, one = exchange(
            (grad[0, 0], grad[1, 0]), (grad[0, 1], grad[1, 1]), (grad[0, 2], grad[1, 2])
        )
        back = jnp.stack([zero[0], one[0], zero[1], one[1], zero[2], one[2]])
        return call(sum_kernel, (2, rows, ncolumns), (True, False), (starts, back))[None]

    in_specs = (
        P("cuts", None, "tile", None),
        P(),
        P("tile", None),
        P("tile"),
        P("tile", None, None),
    )
    out_specs = P("cuts", None, "tile", None)
    return jax.shard_map(local, mesh=mesh, in_specs=in_specs, out_specs=out_specs, check_vma=False)
```

```python
import functools
import math

import jax
import jax.numpy as jnp
import ml_dtypes
import numpy as np
from jax import lax
from jax.experimental import pallas as pl
from jax.experimental.pallas import tpu as pltpu
from jax.sharding import PartitionSpec as P

MESH = pl.DeviceIdType.MESH
LANES = 128


def split_table(table):
    high = table.astype(ml_dtypes.bfloat16)
    low = (table - high.astype(np.float64)).astype(ml_dtypes.bfloat16)
    return np.stack([high, low])


def build_tables(window):
    counter = np.arange(window)
    turned = (counter[:, None] * counter[None, :] % window) * (2.0 * math.pi / window)
    dft = np.exp(-1j * turned) / math.sqrt(window)
    centred = (counter + window // 2) % window - window // 2
    angle = (centred * centred % (4 * window)) * (math.pi / (2 * window))
    prop = (np.conj(dft) * np.exp(-1j * angle)[None, :]) @ dft

    def right(matrix):
        return np.block([[matrix.real, matrix.imag], [-matrix.imag, matrix.real]])

    return np.stack(
        [split_table(m) for w in (dft, prop) for m in (right(w), right(w).T)]
    )


def halves(value):
    high = value.astype(jnp.bfloat16)
    return high, (value - high.astype(jnp.float32)).astype(jnp.bfloat16)


def dot(left, right):
    return jnp.dot(left, right, preferred_element_type=jnp.float32)


def sandwich(real_in, imag_in, table, right, left):
    window = real_in.shape[0]
    high, low = halves(jnp.concatenate([real_in, imag_in], axis=1))
    middle = dot(high, table[right, 0]) + (dot(low, table[right, 0]) + dot(high, table[right, 1]))
    stacked = jnp.concatenate([middle[:, :window], middle[:, window:]], axis=0)
    high, low = halves(stacked)
    final = dot(table[left, 0], high) + (dot(table[left, 0], low) + dot(table[left, 1], high))
    return final[:window], final[window:]


def roll_kernel(rows, pos, probe, rolled):
    core = lax.axis_index("cuts")
    window = probe.shape[1]
    row = jnp.where(core == 0, pos[0, 0], pos[1, 0]) - (lax.axis_index("tile") - 1) * rows
    row = jnp.clip(row, 0, rows)
    turn = jnp.clip(jnp.where(core == 0, pos[0, 1], pos[1, 1]), 0) % window
    for part in range(2):
        rolled[part] = pltpu.roll(pltpu.roll(probe[part], row, 0), turn, 1)


def cut_kernel(strip, starts, *cut):
    blocks = strip.shape[2] // LANES
    lane_row = lax.broadcasted_iota(jnp.int32, (1, LANES), 1)
    for item in range(6):
        start = jnp.full((1, LANES), starts[item], jnp.int32)
        for half in range(2):
            order = list(range(half, blocks, 2))[::-1]
            for part in range(2):
                value = strip[part, :, order[0] * LANES : (order[0] + 1) * LANES]
                for block in order[1:]:
                    value = jnp.where(
                        lane_row + block * LANES >= start,
                        strip[part, :, block * LANES : (block + 1) * LANES],
                        value,
                    )
                cut[item][part, :, half * LANES : (half + 1) * LANES] = value


def wave_kernel(row_ref, live_ref, probe, intensity, table, *pieces):
    win, grad = pieces[:6], pieces[6:]
    rows, window = win[0].shape[1:]
    core = lax.axis_index("cuts")
    row = row_ref[0]
    from_high = lax.broadcasted_iota(jnp.int32, (rows, window), 0) < row

    def object_part(section, part):
        low, own, high = (
            jnp.where(core == section, win[2 * place][part], win[2 * place + 1][part])
            for place in range(3)
        )
        return jnp.concatenate([jnp.where(from_high, high, low), own], axis=0)

    def give_back(section, real_part, imag_part):
        for part, value in ((0, real_part), (1, imag_part)):
            outer = value[:rows]
            parts = (jnp.where(from_high, 0.0, outer), value[rows:], jnp.where(from_high, outer, 0.0))
            for far in range(2):
                @pl.when(core == abs(section - far))
                def _():
                    for place in range(3):
                        grad[2 * place + far][part] = parts[place]

    probe_re, probe_im = probe[0], probe[1]
    obj_re, obj_im = object_part(0, 0), object_part(0, 1)
    wave_re, wave_im = sandwich(
        probe_re * obj_re - probe_im * obj_im, probe_re * obj_im + probe_im * obj_re, table, 2, 3
    )
    obj_re, obj_im = object_part(1, 0), object_part(1, 1)
    far_re, far_im = sandwich(
        wave_re * obj_re - wave_im * obj_im, wave_re * obj_im + wave_im * obj_re, table, 0, 1
    )
    residual = live_ref[0] * (far_re * far_re + far_im * far_im - intensity[...])
    back_re, back_im = sandwich(residual * far_re, residual * far_im, table, 1, 0)
    give_back(1, wave_re * back_re + wave_im * back_im, wave_re * back_im - wave_im * back_re)
    back_re, back_im = sandwich(
        obj_re * back_re + obj_im * back_im, obj_re * back_im - obj_im * back_re, table, 3, 2
    )
    give_back(0, probe_re * back_re + probe_im * back_im, probe_re * back_im - probe_im * back_re)


def sum_kernel(starts, *pieces):
    back, summed = pieces[:6], pieces[6]
    rows, window = back[0].shape[1:]
    blocks = summed.shape[2] // LANES
    lane_row = lax.broadcasted_iota(jnp.int32, (1, LANES), 1)
    for block in range(blocks):
        half = slice((block % 2) * LANES, (block % 2 + 1) * LANES)
        for part in range(2):
            total = jnp.zeros((rows, LANES), jnp.float32)
            for item in range(6):
                offset = lane_row + block * LANES - jnp.full((1, LANES), starts[item], jnp.int32)
                inside = jnp.logical_and(offset >= 0, offset < window)
                total += jnp.where(inside, back[item][part, :, half], 0.0)
            summed[part, :, block * LANES : (block + 1) * LANES] = total


def solution(mesh):
    tiles = mesh.shape["tile"]
    up = [(t, t + 1) for t in range(tiles - 1)]
    down = [(t + 1, t) for t in range(tiles - 1)]
    swap = [(0, 1), (1, 0)]

    def crossed(pairs):
        return [(c * tiles + a, (1 - c) * tiles + b) for c in range(2) for a, b in pairs]

    def call(body, shapes, scalars, arrays):
        return pl.pallas_call(
            body,
            out_shape=[jax.ShapeDtypeStruct(shape, jnp.float32) for shape in shapes],
            in_specs=[
                pl.BlockSpec(memory_space=pltpu.SMEM if index in scalars else pltpu.VMEM)
                for index in range(len(arrays))
            ],
            out_specs=[pl.BlockSpec(memory_space=pltpu.VMEM)] * len(shapes),
            compiler_params=pltpu.CompilerParams(vmem_limit_bytes=40 * 1024 * 1024),
        )(*arrays)

    def exchange(pieces):
        low_same, low_other, own_same, own_other, high_same, high_other = pieces
        both = ("cuts", "tile")
        return (
            lax.ppermute(high_same, "tile", up),
            lax.ppermute(high_other, both, crossed(up)),
            own_same,
            lax.ppermute(own_other, "cuts", swap),
            lax.ppermute(low_same, "tile", down),
            lax.ppermute(low_other, both, crossed(down)),
        )

    def local(object_slices, probe, positions, counts, intensity):
        window = probe.shape[-1]
        rows, ncolumns = object_slices.shape[2:]
        table = jnp.asarray(build_tables(window))
        core = lax.axis_index("cuts")
        below = lax.ppermute(positions, "tile", up)
        above = lax.ppermute(positions, "tile", down)
        around = jnp.stack([below[:, 1], positions[:, 1], above[:, 1]])
        starts = jnp.where(core == 0, around, around[:, ::-1]).reshape(-1)
        piece = (2, rows, window)
        cut = call(cut_kernel, [piece] * 6, (1,), (object_slices[0], starts))
        win = exchange(cut)
        (rolled,) = call(
            functools.partial(roll_kernel, rows), [probe.shape], (0,), (positions, probe)
        )
        row = lax.dynamic_slice(positions[:, 0], (core,), (1,))
        row = row - (lax.axis_index("tile") - 1) * rows
        live = (core < counts).astype(jnp.float32)
        shot = lax.dynamic_index_in_dim(intensity, core, 0, keepdims=False)
        grad = call(wave_kernel, [piece] * 6, (0, 1), (row, live, rolled, shot, table) + win)
        back = exchange(grad)
        return call(sum_kernel, [(2, rows, ncolumns)], (0,), (starts,) + back)[0][None]

    in_specs = (
        P("cuts", None, "tile", None),
        P(),
        P("tile", None),
        P("tile"),
        P("tile", None, None),
    )
    out_specs = P("cuts", None, "tile", None)
    return jax.shard_map(local, mesh=mesh, in_specs=in_specs, out_specs=out_specs, check_vma=False)
```
